32 devices in a mesh: group: 2 (over y), row: 4 (over z), src: 4 (over x, core).
Axes of the slice: x: 2, y: 2, z: 4, core: 2. Of those that a mesh axis runs over, the one named last changes fastest.
Arguments:
- right_side: bfloat16 [5120, 1536], P(('group', 'row'), 'src'), parts along dimension 0, may hold values from -6 to 6
- factor: bfloat16 [5120, 2048], P(('group', 'row')), parts along dimension 0, may hold values from -0.1875 to 0.1875
- pattern: int32 [40, 16], P(('group', 'row')), parts along dimension 0, may hold values 0 or 1
- inverses: bfloat16 [8, 512, 512], P('group', 'src'), parts along dimension 0, may hold values from -4 to 4
- owners: int32 [8], P('group'), parts along dimension 0, may hold values from 0 to 3, as said below
- offsets: int32 [8], P('group'), parts along dimension 0, may hold values from 0 to 1
Outputs:
- solved: bfloat16 [4096, 1536], P(('group', 'row'), 'src'), parts along dimension 0
- updated: bfloat16 [5120, 1536], P(('group', 'row'), 'src'), parts along dimension 0
The draws below stay inside these ranges and needn't reach their ends.
There are 2 independent parts, one for each index of `group`. The reference program is written for one: setup_inputs(seed, part) draws one part's arguments, and reference() takes and returns one part's arrays. A program takes and returns all parts, laid end to end along the dimension named above; each array names one. Nothing has to cross between parts.
Inputs may be any that keep to these rules, and one draw needn't show every extreme that they name: The 4 owners are different row indices, and the first and the last row index are always among them.
All inputs are finite; a program needn't handle non-finite values. No bound on the sum of `pattern` on one device may be relied on, other than what follows from the above.
Results may differ from the reference program's by a relative error of at most 0.0057.
Values may be sent and summed in bfloat16 or wider, within the bound.
No kernel may reach another device: no remote copies, remote signals or barrier semaphores. Data moves between devices by JAX's collectives and lax.ppermute only.
A program may use at most 64 MiB of HBM per device.

```python
import jax
import jax.numpy as jnp
from jax import lax

SN = 4
SNR = 512
BLK = 128
R_DEV = 640
ROWS = 2560
SOURCES = 1536
COLS = 2048
N_ROW = 4


def draw_owners(key, part):
    score_key = jax.random.fold_in(key, 1931)
    order_key = jax.random.fold_in(key, 2711)
    scores = jax.random.randint(score_key, (N_ROW - 2,), 0, 1048576, jnp.int32)
    distinct = scores * N_ROW + jnp.arange(N_ROW - 2, dtype=jnp.int32)
    order = jnp.argsort(distinct, stable=True).astype(jnp.int32)
    middle = order[:SN - 2] + 1
    chosen = jnp.concatenate([jnp.array([0, N_ROW - 1], jnp.int32), middle.astype(jnp.int32)], 0)
    placing = jax.random.permutation(order_key, SN)
    return chosen[placing].astype(jnp.int32)


def draw_inverses(key, part):
    first_key, second_key = jax.random.split(jax.random.fold_in(key, 7), 2)
    diagonal = jax.random.uniform(first_key, (SN, SNR), jnp.float32, 0.6, 1.4)
    noise = jnp.clip(jax.random.normal(second_key, (SN, SNR, SNR), jnp.float32), -4.0, 4.0) * (0.5 / SNR ** 0.5)
    matrix = noise + jnp.eye(SNR, dtype=jnp.float32)[None, :, :] * diagonal[:, :, None]
    return matrix.astype(jnp.bfloat16)


def plant(drawn, rng, smallest, top_value):
    index_at = [jax.random.randint(jax.random.fold_in(rng, axis), (), 0, length) for axis, length in enumerate(drawn.shape)]
    main_axis = drawn.shape.index(max(drawn.shape))
    neighbour = index_at[:main_axis] + [(index_at[main_axis] + 1) % drawn.shape[main_axis]] + index_at[main_axis + 1:]
    return drawn.at[tuple(index_at)].set(smallest).at[tuple(neighbour)].set(top_value)


def shard_levels(rng, shape, shards, smallest, high):
    def one(position, parts):
        steps = jax.random.uniform(jax.random.fold_in(jax.random.fold_in(rng, 6), position), (parts,), jnp.float32, smallest / len(shards), high / len(shards))
        return jnp.repeat(jnp.exp(steps), shape[position] // parts).reshape((-1,) + (1,) * (len(shape) - position - 1))

    gain = one(*shards[0])
    for cut in shards[1:]:
        gain = gain * one(*cut)
    return gain


def centred(stream_key, dims, scale, reach, shards=(), held_as=jnp.bfloat16):
    level = shard_levels(stream_key, dims, shards, -0.22, 0.18) if shards else 1.0
    values = jax.random.normal(stream_key, dims, jnp.float32) * scale * level
    return jnp.minimum(jnp.maximum(values, -reach), reach).astype(held_as)


def setup_inputs(seed: int = 0, part: int = 0) -> dict:
    keys = jax.random.split(jax.random.key(seed), 7)
    own_keys = jax.random.split(jax.random.fold_in(keys[6], part), 7)
    return {
        "right_side": centred(own_keys[0], (ROWS, SOURCES), 1.0, 6.0, ((0, 4), (1, 4))),
        "factor": centred(own_keys[1], (ROWS, COLS), (COLS // 2) ** -0.5, 0.1875, ((0, 4),)),
        "pattern": plant((jax.random.randint(own_keys[2], (ROWS // BLK, COLS // BLK), 0, 2) < 1).astype(jnp.int32), jax.random.fold_in(own_keys[2], 1), 0, 1),
        "inverses": draw_inverses(jax.random.fold_in(jax.random.fold_in(keys[6], part), 71), part),
        "owners": draw_owners(jax.random.fold_in(jax.random.fold_in(keys[6], part), 71), part),
        "offsets": plant(jax.random.randint(own_keys[5], (SN,), 0, R_DEV // BLK - SNR // BLK + 1), jax.random.fold_in(own_keys[5], 1), 0, (R_DEV // BLK - SNR // BLK + 1) - 1).astype(jnp.int32),
    }


def expanded_keep(pattern, ranking, column_node):
    row_blocks, col_blocks = pattern.shape
    tile_mask = jnp.broadcast_to((pattern > 0)[:, None, :, None], (row_blocks, BLK, col_blocks, BLK))
    tile_mask = tile_mask.reshape(row_blocks * BLK, col_blocks * BLK)
    return tile_mask & (ranking[:, None] > column_node[None, :])


def reference(right_side, factor, pattern, inverses, owners, offsets):
    row_index = jnp.arange(ROWS, dtype=jnp.int32)
    starts = (owners * R_DEV + offsets * BLK).astype(jnp.int32)
    ranking = jnp.full((ROWS,), SN, jnp.int32)
    for supernode in range(SN):
        inside = (row_index >= starts[supernode]) & (row_index < starts[supernode] + SNR)
        ranking = jnp.where(inside, jnp.int32(supernode), ranking)
    column_node = (jnp.arange(COLS, dtype=jnp.int32) // SNR).astype(jnp.int32)
    retained = expanded_keep(pattern, ranking, column_node)
    masked = jnp.where(retained, factor, jnp.zeros((), factor.dtype))
    running = right_side.astype(jnp.float32)
    pieces = []
    for supernode in range(SN):
        segment = lax.dynamic_slice(running, (starts[supernode], jnp.int32(0)), (SNR, SOURCES)).astype(jnp.bfloat16)
        solution = jnp.dot(inverses[supernode], segment, preferred_element_type=jnp.float32).astype(jnp.bfloat16)
        pieces.append(solution)
        columns = masked[:, supernode * SNR:(supernode + 1) * SNR]
        running = running - jnp.dot(columns, solution, preferred_element_type=jnp.float32)
    return jnp.concatenate(pieces, 0), running.astype(jnp.bfloat16)
```

```python
import functools

import jax
import jax.numpy as jnp
from jax import lax
from jax.experimental import pallas as pl
from jax.experimental.pallas import tpu as pltpu
from jax.sharding import PartitionSpec as P

SN = 4
SNR = 512
BLK = 128
LEFT = (SN - 1) * SNR
ANY = pl.BlockSpec(memory_space=pl.ANY)
SMEM = pl.BlockSpec(memory_space=pltpu.SMEM)
VMEM = pl.BlockSpec(memory_space=pltpu.VMEM)
PARAMS = pltpu.CompilerParams(vmem_limit_bytes=24 << 20)


def line_gather(value, n):
    slots = [value]
    for chain in range(2):
        got = value
        for hop in range(1, n):
            pairs = []
            for i in range(n):
                side = 1 if (i + chain + hop) % 2 else -1
                if 0 <= i + side * hop < n:
                    pairs.append((i + side, i))
            got = lax.ppermute(got, "row", pairs) if pairs else None
            slots.append(got)
    return slots


def slot_of(owner, n):
    position = lax.axis_index("row")
    away = owner - position
    hop = jnp.abs(away)
    side = jnp.where(away > 0, 1, 0)
    chain = lax.rem(position + hop + side, 2)
    return jnp.where(away == 0, 0, hop + chain * (n - 1))


def src_gather(value, n):
    pieces = {0: value}
    bit = n // 2
    while bit:
        for distance in list(pieces):
            pieces[distance ^ bit] = lax.ppermute(
                pieces[distance], "src", [(i, i ^ bit) for i in range(n)]
            )
        bit //= 2
    return [pieces[d] for d in range(n)]


def own_start(owners, offsets):
    position = lax.axis_index("row")
    start = jnp.int32(0)
    for node in range(SN):
        start = jnp.where(owners[node] == position, offsets[node] * BLK, start)
    return start


def start_matching(slots, wanted, place):
    for index, slot in enumerate(slots):
        if slot is not None:

            @pl.when(wanted == index)
            def _(slot=slot):
                place(slot).start()


def fill(held, refs):
    refs = iter(refs)
    return [next(refs) if there else None for there in held]


def stage_kernel(quarter, owners, offsets, pattern, factor, right, piece, segment, rows, sems):
    start = pl.multiple_of(own_start(owners, offsets), BLK)
    first = pl.multiple_of(start + lax.axis_index("src") * quarter, quarter)
    fetch = pltpu.make_async_copy(factor.at[pl.ds(first, quarter), pl.ds(0, LEFT)], rows, sems.at[0])
    move = pltpu.make_async_copy(right.at[pl.ds(start, SNR)], segment, sems.at[1])
    fetch.start()
    move.start()
    fetch.wait()
    tall = min(quarter, BLK)
    for top in range(0, quarter, tall):
        tile_row = (first + top) // BLK
        for col in range(0, LEFT, BLK):
            tile = rows[top : top + tall, col : col + BLK]
            kept = jnp.where(pattern[tile_row, col // BLK] > 0, tile, jnp.zeros_like(tile))
            piece[top : top + tall, col : col + BLK] = kept
    move.wait()


def stage(owners, offsets, pattern, factor, right, n_src):
    quarter = SNR // n_src
    shapes = [(quarter, LEFT), (SNR, right.shape[1])]
    return pl.pallas_call(
        functools.partial(stage_kernel, quarter),
        out_shape=[jax.ShapeDtypeStruct(shape, jnp.bfloat16) for shape in shapes],
        in_specs=[SMEM] * 3 + [ANY] * 2,
        out_specs=[VMEM, VMEM],
        scratch_shapes=[
            pltpu.VMEM((quarter, LEFT), jnp.bfloat16),
            pltpu.SemaphoreType.DMA((2,)),
        ],
        compiler_params=pltpu.CompilerParams(vmem_limit_bytes=56 << 20),
        name="stage",
    )(owners, offsets, pattern, factor, right)


def pick_kernel(n_row, held, owners, *refs):
    slots = fill(held, refs[: sum(held)])
    near, far, sems = refs[sum(held) :]

    def place(node, slot):
        width = node * SNR
        first = 0 if node == SN - 1 else node * (node - 1) // 2 * SNR
        target = (far if node == SN - 1 else near).at[:, pl.ds(first, width)]
        return pltpu.make_async_copy(slot.at[:, pl.ds(0, width)], target, sems.at[node])

    for node in range(1, SN):
        start_matching(slots, slot_of(owners[node], n_row), functools.partial(place, node))
    for node in range(1, SN):
        place(node, slots[0]).wait()


def pick(owners, slots, n_row):
    held = [slot is not None for slot in slots]
    quarter = slots[0].shape[0]
    shapes = [(quarter, (SN - 1) * (SN - 2) // 2 * SNR), (quarter, LEFT)]
    return pl.pallas_call(
        functools.partial(pick_kernel, n_row, held),
        out_shape=[jax.ShapeDtypeStruct(shape, jnp.bfloat16) for shape in shapes],
        in_specs=[SMEM] + [ANY] * sum(held),
        out_specs=[ANY] * 2,
        scratch_shapes=[pltpu.SemaphoreType.DMA((SN,))],
        compiler_params=PARAMS,
        name="pick",
    )(owners, *(slot for slot in slots if slot is not None))


def order_kernel(n_row, held, owners, *refs):
    slots = fill(held, refs[: sum(held)])
    segments, sems = refs[sum(held) :]

    def place(node, slot):
        return pltpu.make_async_copy(slot, segments.at[node], sems.at[node])

    for node in range(SN):
        start_matching(slots, slot_of(owners[node], n_row), functools.partial(place, node))
    for node in range(SN):
        place(node, slots[0]).wait()


def order(owners, slots, n_row):
    held = [slot is not None for slot in slots]
    return pl.pallas_call(
        functools.partial(order_kernel, n_row, held),
        out_shape=jax.ShapeDtypeStruct((SN,) + slots[0].shape, jnp.bfloat16),
        in_specs=[SMEM] + [ANY] * sum(held),
        out_specs=ANY,
        scratch_shapes=[pltpu.SemaphoreType.DMA((SN,))],
        compiler_params=PARAMS,
        cost_estimate=pl.CostEstimate(flops=24 * 10**9, bytes_accessed=0, transcendentals=0),
        name="order",
    )(owners, *(slot for slot in slots if slot is not None))


def join_kernel(*refs):
    *pieces, whole, sems = refs
    me, quarter = lax.axis_index("src"), SNR // len(pieces)
    copies = []
    for d, piece in enumerate(pieces):
        rows = pl.ds(pl.multiple_of(jnp.bitwise_xor(me, d) * quarter, quarter), quarter)
        place = whole.at[rows] if len(whole.shape) == 2 else whole.at[:, rows]
        copies.append(pltpu.make_async_copy(piece, place, sems.at[d]))
    for copy in copies:
        copy.start()
    for copy in copies:
        copy.wait()


def join(pieces):
    shape = pieces[0].shape[:-2] + (SNR, pieces[0].shape[-1])
    return pl.pallas_call(
        join_kernel,
        out_shape=jax.ShapeDtypeStruct(shape, jnp.bfloat16),
        in_specs=[ANY] * len(pieces),
        out_specs=ANY,
        scratch_shapes=[pltpu.SemaphoreType.DMA((len(pieces),))],
        compiler_params=PARAMS,
        name="join",
    )(*pieces)


def mask_kernel(owners, offsets, pattern, factor, masked):
    start = own_start(owners, offsets)
    position = lax.axis_index("row")
    owned = jnp.int32(SN)
    for node in range(SN):
        owned = jnp.where(owners[node] == position, node, owned)
    for top in range(0, factor.shape[0], BLK):
        rank = jnp.where((top >= start) & (top < start + SNR), owned, SN)
        for col in range(0, factor.shape[1], BLK):
            keep = (pattern[top // BLK, col // BLK] > 0) & (rank > col // SNR)
            tile = factor[top : top + BLK, col : col + BLK]
            masked[top : top + BLK, col : col + BLK] = jnp.where(keep, tile, jnp.zeros_like(tile))


def mask(owners, offsets, pattern, factor):
    return pl.pallas_call(
        mask_kernel,
        out_shape=jax.ShapeDtypeStruct(factor.shape, factor.dtype),
        in_specs=[SMEM] * 3 + [pl.BlockSpec(memory_space=pltpu.VMEM)],
        out_specs=pl.BlockSpec(memory_space=pltpu.VMEM),
        compiler_params=PARAMS,
        name="mask",
    )(owners, offsets, pattern, factor)


def solve_kernel(owners, inverse, segments, near, far, masked, right, solved, updated, xs, out, sems):
    position = lax.axis_index("row")
    for node in range(SN):
        segment = segments[node]
        if node:
            first = node * (node - 1) // 2 * SNR
            lower = far[...] if node == SN - 1 else near[:, first : first + node * SNR]
            update = jnp.dot(lower, xs[: node * SNR], preferred_element_type=jnp.float32)
            segment = (segment.astype(jnp.float32) - update).astype(jnp.bfloat16)
        x = jnp.dot(inverse[node], segment, preferred_element_type=jnp.float32)
        xs[node * SNR : (node + 1) * SNR] = x.astype(jnp.bfloat16)
    out_rows = solved.shape[0]
    solved_copy = pltpu.make_async_copy(
        xs.at[pl.ds(pl.multiple_of(position * out_rows, out_rows), out_rows)], solved, sems.at[0]
    )
    solved_copy.start()
    update = jnp.dot(masked[...], xs[...], preferred_element_type=jnp.float32)
    out[...] = (right[...].astype(jnp.float32) - update).astype(jnp.bfloat16)
    updated_copy = pltpu.make_async_copy(out, updated, sems.at[1])
    updated_copy.start()
    solved_copy.wait()
    updated_copy.wait()


def solve(owners, inverse, segments, near, far, masked, right, n_row):
    rows, columns = right.shape
    return pl.pallas_call(
        solve_kernel,
        out_shape=(
            jax.ShapeDtypeStruct((SN * SNR // n_row, columns), jnp.bfloat16),
            jax.ShapeDtypeStruct((rows, columns), jnp.bfloat16),
        ),
        in_specs=[SMEM] + [VMEM] * 6,
        out_specs=(ANY, ANY),
        scratch_shapes=[
            pltpu.VMEM((SN * SNR, columns), jnp.bfloat16),
            pltpu.VMEM((rows, columns), jnp.bfloat16),
            pltpu.SemaphoreType.DMA((2,)),
        ],
        compiler_params=PARAMS,
        name="solve",
    )(owners, inverse, segments, near, far, masked, right)


def on_device(right_side, factor, pattern, inverses, owners, offsets):
    n_row, n_src = lax.axis_size("row"), lax.axis_size("src")
    piece, segment = stage(owners, offsets, pattern, factor, right_side, n_src)
    pieces = line_gather(piece, n_row)
    inverse = join(src_gather(inverses, n_src))
    near, far = pick(owners, pieces, n_row)
    near, far, inverse = lax.optimization_barrier((near, far, inverse))
    near, far = join(src_gather(near, n_src)), join(src_gather(far, n_src))
    segments = order(owners, line_gather(segment, n_row), n_row)
    masked = mask(owners, offsets, pattern, factor)
    return solve(owners, inverse, segments, near, far, masked, right_side, n_row)


def solution(mesh):
    placed = (
        P(("group", "row"), "src"),
        P(("group", "row"), None),
        P(("group", "row"), None),
        P("group", "src", None),
        P("group"),
        P("group"),
    )
    return jax.shard_map(
        on_device,
        mesh=mesh,
        in_specs=placed,
        out_specs=(P(("group", "row"), "src"), P(("group", "row"), "src")),
        check_vma=False,
    )
```

```python
import functools

import jax
import jax.numpy as jnp
from jax import lax
from jax.experimental import pallas as pl
from jax.experimental.pallas import tpu as pltpu
from jax.sharding import PartitionSpec as P

SN = 4
SNR = 512
BLK = 128
LEFT = (SN - 1) * SNR
ANY = pl.BlockSpec(memory_space=pl.ANY)
SMEM = pl.BlockSpec(memory_space=pltpu.SMEM)
VMEM = pl.BlockSpec(memory_space=pltpu.VMEM)
PARAMS = pltpu.CompilerParams(vmem_limit_bytes=24 << 20)


def line_gather(value, n):
    slots = [value]
    for chain in range(2):
        got = value
        for hop in range(1, n):
            pairs = []
            for i in range(n):
                side = 1 if (i + chain + hop) % 2 else -1
                if 0 <= i + side * hop < n:
                    pairs.append((i + side, i))
            got = lax.ppermute(got, "row", pairs) if pairs else None
            slots.append(got)
    return slots


def slot_of(owner, n):
    position = lax.axis_index("row")
    away = owner - position
    hop = jnp.abs(away)
    side = jnp.where(away > 0, 1, 0)
    chain = lax.rem(position + hop + side, 2)
    return jnp.where(away == 0, 0, hop + chain * (n - 1))


def src_gather(value, n):
    pieces = {0: value}
    bit = n // 2
    while bit:
        for distance in list(pieces):
            pieces[distance ^ bit] = lax.ppermute(
                pieces[distance], "src", [(i, i ^ bit) for i in range(n)]
            )
        bit //= 2
    return [pieces[d] for d in range(n)]


def own_start(owners, offsets):
    position = lax.axis_index("row")
    start = jnp.int32(0)
    for node in range(SN):
        start = jnp.where(owners[node] == position, offsets[node] * BLK, start)
    return start


def start_matching(slots, wanted, place):
    for index, slot in enumerate(slots):
        if slot is not None:

            @pl.when(wanted == index)
            def _(slot=slot):
                place(slot).start()


def fill(held, refs):
    refs = iter(refs)
    return [next(refs) if there else None for there in held]


def stage_kernel(quarter, owners, offsets, pattern, factor, right, piece, segment, rows, sems):
    start = pl.multiple_of(own_start(owners, offsets), BLK)
    first = pl.multiple_of(start + lax.axis_index("src") * quarter, quarter)
    fetch = pltpu.make_async_copy(factor.at[pl.ds(first, quarter), pl.ds(0, LEFT)], rows, sems.at[0])
    move = pltpu.make_async_copy(right.at[pl.ds(start, SNR)], segment, sems.at[1])
    fetch.start()
    move.start()
    fetch.wait()
    tall = min(quarter, BLK)
    for top in range(0, quarter, tall):
        tile_row = (first + top) // BLK
        for col in range(0, LEFT, BLK):
            tile = rows[top : top + tall, col : col + BLK]
            kept = jnp.where(pattern[tile_row, col // BLK] > 0, tile, jnp.zeros_like(tile))
            piece[top : top + tall, col : col + BLK] = kept
    move.wait()


def stage(owners, offsets, pattern, factor, right, n_src):
    quarter = SNR // n_src
    shapes = [(quarter, LEFT), (SNR, right.shape[1])]
    return pl.pallas_call(
        functools.partial(stage_kernel, quarter),
        out_shape=[jax.ShapeDtypeStruct(shape, jnp.bfloat16) for shape in shapes],
        in_specs=[SMEM] * 3 + [ANY] * 2,
        out_specs=[VMEM, VMEM],
        scratch_shapes=[
            pltpu.VMEM((quarter, LEFT), jnp.bfloat16),
            pltpu.SemaphoreType.DMA((2,)),
        ],
        compiler_params=pltpu.CompilerParams(vmem_limit_bytes=56 << 20),
        name="stage",
    )(owners, offsets, pattern, factor, right)


def pick_kernel(n_row, held, owners, *refs):
    slots = fill(held, refs[: sum(held)])
    near, far, sems = refs[sum(held) :]

    def place(node, slot):
        width = node * SNR
        first = 0 if node == SN - 1 else node * (node - 1) // 2 * SNR
        target = (far if node == SN - 1 else near).at[:, pl.ds(first, width)]
        return pltpu.make_async_copy(slot.at[:, pl.ds(0, width)], target, sems.at[node])

    for node in range(1, SN):
        start_matching(slots, slot_of(owners[node], n_row), functools.partial(place, node))
    for node in range(1, SN):
        place(node, slots[0]).wait()


def pick(owners, slots, n_row):
    held = [slot is not None for slot in slots]
    quarter = slots[0].shape[0]
    shapes = [(quarter, (SN - 1) * (SN - 2) // 2 * SNR), (quarter, LEFT)]
    return pl.pallas_call(
        functools.partial(pick_kernel, n_row, held),
        out_shape=[jax.ShapeDtypeStruct(shape, jnp.bfloat16) for shape in shapes],
        in_specs=[SMEM] + [ANY] * sum(held),
        out_specs=[ANY] * 2,
        scratch_shapes=[pltpu.SemaphoreType.DMA((SN,))],
        compiler_params=PARAMS,
        name="pick",
    )(owners, *(slot for slot in slots if slot is not None))


def join_kernel(*refs):
    *pieces, whole, sems = refs
    me, quarter = lax.axis_index("src"), SNR // len(pieces)
    copies = []
    for d, piece in enumerate(pieces):
        rows = pl.ds(pl.multiple_of(jnp.bitwise_xor(me, d) * quarter, quarter), quarter)
        place = whole.at[rows] if len(whole.shape) == 2 else whole.at[:, rows]
        copies.append(pltpu.make_async_copy(piece, place, sems.at[d]))
    for copy in copies:
        copy.start()
    for copy in copies:
        copy.wait()


def join(pieces):
    shape = pieces[0].shape[:-2] + (SNR, pieces[0].shape[-1])
    return pl.pallas_call(
        join_kernel,
        out_shape=jax.ShapeDtypeStruct(shape, jnp.bfloat16),
        in_specs=[ANY] * len(pieces),
        out_specs=ANY,
        scratch_shapes=[pltpu.SemaphoreType.DMA((len(pieces),))],
        compiler_params=PARAMS,
        name="join",
    )(*pieces)


def mask_kernel(owners, offsets, pattern, factor, masked):
    start = own_start(owners, offsets)
    position = lax.axis_index("row")
    owned = jnp.int32(SN)
    for node in range(SN):
        owned = jnp.where(owners[node] == position, node, owned)
    for top in range(0, factor.shape[0], BLK):
        rank = jnp.where((top >= start) & (top < start + SNR), owned, SN)
        for col in range(0, factor.shape[1], BLK):
            keep = (pattern[top // BLK, col // BLK] > 0) & (rank > col // SNR)
            tile = factor[top : top + BLK, col : col + BLK]
            masked[top : top + BLK, col : col + BLK] = jnp.where(keep, tile, jnp.zeros_like(tile))


def mask(owners, offsets, pattern, factor):
    return pl.pallas_call(
        mask_kernel,
        out_shape=jax.ShapeDtypeStruct(factor.shape, factor.dtype),
        in_specs=[SMEM] * 3 + [pl.BlockSpec(memory_space=pltpu.VMEM)],
        out_specs=pl.BlockSpec(memory_space=pltpu.VMEM),
        compiler_params=PARAMS,
        name="mask",
    )(owners, offsets, pattern, factor)


def first_kernel(n_row, held, owners, inverse, masked, right, *refs):
    slots = fill(held, refs[: sum(held)])
    segments, solution, total, segment, sems = refs[sum(held) :]

    def place(node, slot):
        target = segments.at[node - 1] if node else segment
        return pltpu.make_async_copy(slot, target, sems.at[node])

    for node in range(SN):
        start_matching(slots, slot_of(owners[node], n_row), functools.partial(place, node))
    place(0, slots[0]).wait()
    x = jnp.dot(inverse[0], segment[...], preferred_element_type=jnp.float32).astype(jnp.bfloat16)
    solution[...] = x
    update = jnp.dot(masked[:, :SNR], x, preferred_element_type=jnp.float32)
    total[...] = right[...].astype(jnp.float32) - update
    for node in range(1, SN):
        place(node, slots[0]).wait()


def first(owners, inverse, masked, right, slots, n_row):
    held = [slot is not None for slot in slots]
    rows, columns = right.shape
    return pl.pallas_call(
        functools.partial(first_kernel, n_row, held),
        out_shape=(
            jax.ShapeDtypeStruct((SN - 1, SNR, columns), jnp.bfloat16),
            jax.ShapeDtypeStruct((SNR, columns), jnp.bfloat16),
            jax.ShapeDtypeStruct((rows, columns), jnp.float32),
        ),
        in_specs=[SMEM] + [VMEM] * 3 + [ANY] * sum(held),
        out_specs=(ANY, VMEM, VMEM),
        scratch_shapes=[
            pltpu.VMEM((SNR, columns), jnp.bfloat16),
            pltpu.SemaphoreType.DMA((SN,)),
        ],
        compiler_params=PARAMS,
        cost_estimate=pl.CostEstimate(flops=60 * 10**9, bytes_accessed=0, transcendentals=0),
        name="first",
    )(owners, inverse, masked, right, *(slot for slot in slots if slot is not None))


def middle_kernel(inverse, near, masked, segments, start, before, solutions, total):
    left = before[...]
    for node in range(1, SN - 1):
        at = node * (node - 1) // 2 * SNR
        update = jnp.dot(near[:, at : at + SNR], start[...], preferred_element_type=jnp.float32)
        if node > 1:
            update += jnp.dot(
                near[:, at + SNR : at + node * SNR],
                solutions[: (node - 1) * SNR],
                preferred_element_type=jnp.float32,
            )
        segment = (segments[node - 1].astype(jnp.float32) - update).astype(jnp.bfloat16)
        x = jnp.dot(inverse[node], segment, preferred_element_type=jnp.float32).astype(jnp.bfloat16)
        solutions[(node - 1) * SNR : node * SNR] = x
    cols = masked[:, SNR : (SN - 1) * SNR]
    total[...] = left - jnp.dot(cols, solutions[...], preferred_element_type=jnp.float32)


def middle(inverse, near, masked, segments, start, total):
    columns = start.shape[1]
    return pl.pallas_call(
        middle_kernel,
        out_shape=(
            jax.ShapeDtypeStruct(((SN - 2) * SNR, columns), jnp.bfloat16),
            jax.ShapeDtypeStruct(total.shape, jnp.float32),
        ),
        in_specs=[VMEM] * 6,
        out_specs=(VMEM, VMEM),
        compiler_params=PARAMS,
        cost_estimate=pl.CostEstimate(flops=24 * 10**9, bytes_accessed=0, transcendentals=0),
        name="middle",
    )(inverse, near, masked, segments, start, total)


def last_kernel(inverse, far, masked, segments, start, solutions, total, solved, updated, xs, out, sems):
    position = lax.axis_index("row")
    last = (SN - 1) * SNR
    moves = [
        pltpu.make_async_copy(start, xs.at[pl.ds(0, SNR)], sems.at[0]),
        pltpu.make_async_copy(solutions, xs.at[pl.ds(SNR, last - SNR)], sems.at[1]),
    ]
    for move in moves:
        move.start()
    update = jnp.dot(far[:, :SNR], start[...], preferred_element_type=jnp.float32)
    update += jnp.dot(far[:, SNR:], solutions[...], preferred_element_type=jnp.float32)
    segment = (segments[SN - 2].astype(jnp.float32) - update).astype(jnp.bfloat16)
    x = jnp.dot(inverse[SN - 1], segment, preferred_element_type=jnp.float32).astype(jnp.bfloat16)
    xs[last:] = x
    for move in moves:
        move.wait()
    out_rows = solved.shape[0]
    solved_copy = pltpu.make_async_copy(
        xs.at[pl.ds(pl.multiple_of(position * out_rows, out_rows), out_rows)], solved, sems.at[0]
    )
    solved_copy.start()
    update = jnp.dot(masked[:, last:], x, preferred_element_type=jnp.float32)
    out[...] = (total[...] - update).astype(jnp.bfloat16)
    updated_copy = pltpu.make_async_copy(out, updated, sems.at[1])
    updated_copy.start()
    solved_copy.wait()
    updated_copy.wait()


def last(inverse, far, masked, segments, start, solutions, total, n_row):
    rows, columns = total.shape
    return pl.pallas_call(
        last_kernel,
        out_shape=(
            jax.ShapeDtypeStruct((SN * SNR // n_row, columns), jnp.bfloat16),
            jax.ShapeDtypeStruct((rows, columns), jnp.bfloat16),
        ),
        in_specs=[VMEM] * 7,
        out_specs=(ANY, ANY),
        scratch_shapes=[
            pltpu.VMEM((SN * SNR, columns), jnp.bfloat16),
            pltpu.VMEM((rows, columns), jnp.bfloat16),
            pltpu.SemaphoreType.DMA((2,)),
        ],
        compiler_params=PARAMS,
        name="last",
    )(inverse, far, masked, segments, start, solutions, total)


def on_device(right_side, factor, pattern, inverses, owners, offsets):
    n_row, n_src = lax.axis_size("row"), lax.axis_size("src")
    piece, segment = stage(owners, offsets, pattern, factor, right_side, n_src)
    pieces = line_gather(piece, n_row)
    inverse = join(src_gather(inverses, n_src))
    near, far = pick(owners, pieces, n_row)
    near, far, inverse = lax.optimization_barrier((near, far, inverse))
    near, far = join(src_gather(near, n_src)), join(src_gather(far, n_src))
    masked = mask(owners, offsets, pattern, factor)
    slots = line_gather(segment, n_row)
    segments, start, total = first(owners, inverse, masked, right_side, slots, n_row)
    solutions, total = middle(inverse, near, masked, segments, start, total)
    return last(inverse, far, masked, segments, start, solutions, total, n_row)


def solution(mesh):
    placed = (
        P(("group", "row"), "src"),
        P(("group", "row"), None),
        P(("group", "row"), None),
        P("group", "src", None),
        P("group"),
        P("group"),
    )
    return jax.shard_map(
        on_device,
        mesh=mesh,
        in_specs=placed,
        out_specs=(P(("group", "row"), "src"), P(("group", "row"), "src")),
        check_vma=False,
    )
```

```python
import functools

import jax
import jax.numpy as jnp
from jax import lax
from jax.experimental import pallas as pl
from jax.experimental.pallas import tpu as pltpu
from jax.sharding import PartitionSpec as P

SN = 4
SNR = 512
BLK = 128
LEFT = (SN - 1) * SNR
ANY = pl.BlockSpec(memory_space=pl.ANY)
SMEM = pl.BlockSpec(memory_space=pltpu.SMEM)
VMEM = pl.BlockSpec(memory_space=pltpu.VMEM)
PARAMS = pltpu.CompilerParams(vmem_limit_bytes=24 << 20)


def line_gather(value, n):
    slots = [value]
    for chain in range(2):
        got = value
        for hop in range(1, n):
            pairs = []
            for i in range(n):
                side = 1 if (i + chain + hop) % 2 else -1
                there, back = i + side * hop, i - side * (hop - 1)
                if 0 <= i + side < n and (0 <= there < n or 0 <= back < n):
                    pairs.append((i + side, i))
            got = lax.ppermute(got, "row", pairs) if pairs else None
            slots.append(got)
    return slots


def slot_of(owner, n):
    position = lax.axis_index("row")
    away = owner - position
    hop = jnp.abs(away)
    side = jnp.where(away > 0, 1, 0)
    chain = lax.rem(position + hop + side, 2)
    return jnp.where(away == 0, 0, hop + chain * (n - 1))


def src_gather(value, n):
    pieces = {0: value}
    bit = n // 2
    while bit:
        for distance in list(pieces):
            pieces[distance ^ bit] = lax.ppermute(
                pieces[distance], "src", [(i, i ^ bit) for i in range(n)]
            )
        bit //= 2
    return [pieces[d] for d in range(n)]


def own_start(owners, offsets):
    position = lax.axis_index("row")
    start = jnp.int32(0)
    for node in range(SN):
        start = jnp.where(owners[node] == position, offsets[node] * BLK, start)
    return start


def start_matching(slots, wanted, place):
    for index, slot in enumerate(slots):
        if slot is not None:

            @pl.when(wanted == index)
            def _(slot=slot):
                place(slot).start()


def fill(held, refs):
    refs = iter(refs)
    return [next(refs) if there else None for there in held]


def stage_kernel(quarter, owners, offsets, pattern, factor, right, piece, segment, rows, sems):
    start = pl.multiple_of(own_start(owners, offsets), BLK)
    first = pl.multiple_of(start + lax.axis_index("src") * quarter, quarter)
    fetch = pltpu.make_async_copy(factor.at[pl.ds(first, quarter), pl.ds(0, LEFT)], rows, sems.at[0])
    move = pltpu.make_async_copy(right.at[pl.ds(start, SNR)], segment, sems.at[1])
    fetch.start()
    move.start()
    fetch.wait()
    tall = min(quarter, BLK)
    for top in range(0, quarter, tall):
        tile_row = (first + top) // BLK
        for col in range(0, LEFT, BLK):
            tile = rows[top : top + tall, col : col + BLK]
            kept = jnp.where(pattern[tile_row, col // BLK] > 0, tile, jnp.zeros_like(tile))
            piece[top : top + tall, col : col + BLK] = kept
    move.wait()


def stage(owners, offsets, pattern, factor, right, n_src):
    quarter = SNR // n_src
    shapes = [(quarter, LEFT), (SNR, right.shape[1])]
    return pl.pallas_call(
        functools.partial(stage_kernel, quarter),
        out_shape=[jax.ShapeDtypeStruct(shape, jnp.bfloat16) for shape in shapes],
        in_specs=[SMEM] * 3 + [ANY] * 2,
        out_specs=[VMEM, VMEM],
        scratch_shapes=[
            pltpu.VMEM((quarter, LEFT), jnp.bfloat16),
            pltpu.SemaphoreType.DMA((2,)),
        ],
        compiler_params=pltpu.CompilerParams(vmem_limit_bytes=56 << 20),
        name="stage",
    )(owners, offsets, pattern, factor, right)


def pick_kernel(n_row, held, owners, *refs):
    slots = fill(held, refs[: sum(held)])
    near, far, sems = refs[sum(held) :]

    def place(node, slot):
        width = node * SNR
        first = 0 if node == SN - 1 else node * (node - 1) // 2 * SNR
        target = (far if node == SN - 1 else near).at[:, pl.ds(first, width)]
        return pltpu.make_async_copy(slot.at[:, pl.ds(0, width)], target, sems.at[node])

    for node in range(1, SN):
        start_matching(slots, slot_of(owners[node], n_row), functools.partial(place, node))
    for node in range(1, SN):
        place(node, slots[0]).wait()


def pick(owners, slots, n_row):
    held = [slot is not None for slot in slots]
    quarter = slots[0].shape[0]
    shapes = [(quarter, (SN - 1) * (SN - 2) // 2 * SNR), (quarter, LEFT)]
    return pl.pallas_call(
        functools.partial(pick_kernel, n_row, held),
        out_shape=[jax.ShapeDtypeStruct(shape, jnp.bfloat16) for shape in shapes],
        in_specs=[SMEM] + [ANY] * sum(held),
        out_specs=[ANY] * 2,
        scratch_shapes=[pltpu.SemaphoreType.DMA((SN,))],
        compiler_params=PARAMS,
        name="pick",
    )(owners, *(slot for slot in slots if slot is not None))


def join_kernel(*refs):
    *pieces, whole, sems = refs
    me, quarter = lax.axis_index("src"), SNR // len(pieces)
    copies = []
    for d, piece in enumerate(pieces):
        rows = pl.ds(pl.multiple_of(jnp.bitwise_xor(me, d) * quarter, quarter), quarter)
        place = whole.at[rows] if len(whole.shape) == 2 else whole.at[:, rows]
        copies.append(pltpu.make_async_copy(piece, place, sems.at[d]))
    for copy in copies:
        copy.start()
    for copy in copies:
        copy.wait()


def join(pieces):
    shape = pieces[0].shape[:-2] + (SNR, pieces[0].shape[-1])
    return pl.pallas_call(
        join_kernel,
        out_shape=jax.ShapeDtypeStruct(shape, jnp.bfloat16),
        in_specs=[ANY] * len(pieces),
        out_specs=ANY,
        scratch_shapes=[pltpu.SemaphoreType.DMA((len(pieces),))],
        compiler_params=PARAMS,
        name="join",
    )(*pieces)


def mask_kernel(owners, offsets, pattern, factor, masked):
    start = own_start(owners, offsets)
    position = lax.axis_index("row")
    owned = jnp.int32(SN)
    for node in range(SN):
        owned = jnp.where(owners[node] == position, node, owned)
    for top in range(0, factor.shape[0], BLK):
        rank = jnp.where((top >= start) & (top < start + SNR), owned, SN)
        for col in range(0, factor.shape[1], BLK):
            keep = (pattern[top // BLK, col // BLK] > 0) & (rank > col // SNR)
            tile = factor[top : top + BLK, col : col + BLK]
            masked[top : top + BLK, col : col + BLK] = jnp.where(keep, tile, jnp.zeros_like(tile))


def mask(owners, offsets, pattern, factor):
    return pl.pallas_call(
        mask_kernel,
        out_shape=jax.ShapeDtypeStruct(factor.shape, factor.dtype),
        in_specs=[SMEM] * 3 + [pl.BlockSpec(memory_space=pltpu.VMEM)],
        out_specs=pl.BlockSpec(memory_space=pltpu.VMEM),
        compiler_params=PARAMS,
        name="mask",
    )(owners, offsets, pattern, factor)


def first_kernel(n_row, held, owners, inverse, masked, right, *refs):
    slots = fill(held, refs[: sum(held)])
    segments, solution, total, segment, sems = refs[sum(held) :]

    def place(node, slot):
        target = segments.at[node - 1] if node else segment
        return pltpu.make_async_copy(slot, target, sems.at[node])

    for node in range(SN):
        start_matching(slots, slot_of(owners[node], n_row), functools.partial(place, node))
    place(0, slots[0]).wait()
    x = jnp.dot(inverse[0], segment[...], preferred_element_type=jnp.float32).astype(jnp.bfloat16)
    solution[...] = x
    update = jnp.dot(masked[:, :SNR], x, preferred_element_type=jnp.float32)
    total[...] = right[...].astype(jnp.float32) - update
    for node in range(1, SN):
        place(node, slots[0]).wait()


def first(owners, inverse, masked, right, slots, n_row):
    held = [slot is not None for slot in slots]
    rows, columns = right.shape
    return pl.pallas_call(
        functools.partial(first_kernel, n_row, held),
        out_shape=(
            jax.ShapeDtypeStruct((SN - 1, SNR, columns), jnp.bfloat16),
            jax.ShapeDtypeStruct((SNR, columns), jnp.bfloat16),
            jax.ShapeDtypeStruct((rows, columns), jnp.float32),
        ),
        in_specs=[SMEM] + [VMEM] * 3 + [ANY] * sum(held),
        out_specs=(ANY, VMEM, VMEM),
        scratch_shapes=[
            pltpu.VMEM((SNR, columns), jnp.bfloat16),
            pltpu.SemaphoreType.DMA((SN,)),
        ],
        compiler_params=PARAMS,
        cost_estimate=pl.CostEstimate(flops=60 * 10**9, bytes_accessed=0, transcendentals=0),
        name="first",
    )(owners, inverse, masked, right, *(slot for slot in slots if slot is not None))


def middle_kernel(inverse, near, masked, segments, start, before, solutions, total):
    left = before[...]
    for node in range(1, SN - 1):
        at = node * (node - 1) // 2 * SNR
        update = jnp.dot(near[:, at : at + SNR], start[...], preferred_element_type=jnp.float32)
        if node > 1:
            update += jnp.dot(
                near[:, at + SNR : at + node * SNR],
                solutions[: (node - 1) * SNR],
                preferred_element_type=jnp.float32,
            )
        segment = (segments[node - 1].astype(jnp.float32) - update).astype(jnp.bfloat16)
        x = jnp.dot(inverse[node], segment, preferred_element_type=jnp.float32).astype(jnp.bfloat16)
        solutions[(node - 1) * SNR : node * SNR] = x
    cols = masked[:, SNR : (SN - 1) * SNR]
    total[...] = left - jnp.dot(cols, solutions[...], preferred_element_type=jnp.float32)


def middle(inverse, near, masked, segments, start, total):
    columns = start.shape[1]
    return pl.pallas_call(
        middle_kernel,
        out_shape=(
            jax.ShapeDtypeStruct(((SN - 2) * SNR, columns), jnp.bfloat16),
            jax.ShapeDtypeStruct(total.shape, jnp.float32),
        ),
        in_specs=[VMEM] * 6,
        out_specs=(VMEM, VMEM),
        compiler_params=PARAMS,
        cost_estimate=pl.CostEstimate(flops=24 * 10**9, bytes_accessed=0, transcendentals=0),
        name="middle",
    )(inverse, near, masked, segments, start, total)


def last_kernel(inverse, far, masked, segments, start, solutions, total, solved, updated, xs, out, sems):
    position = lax.axis_index("row")
    last = (SN - 1) * SNR
    moves = [
        pltpu.make_async_copy(start, xs.at[pl.ds(0, SNR)], sems.at[0]),
        pltpu.make_async_copy(solutions, xs.at[pl.ds(SNR, last - SNR)], sems.at[1]),
    ]
    for move in moves:
        move.start()
    update = jnp.dot(far[:, :SNR], start[...], preferred_element_type=jnp.float32)
    update += jnp.dot(far[:, SNR:], solutions[...], preferred_element_type=jnp.float32)
    segment = (segments[SN - 2].astype(jnp.float32) - update).astype(jnp.bfloat16)
    x = jnp.dot(inverse[SN - 1], segment, preferred_element_type=jnp.float32).astype(jnp.bfloat16)
    xs[last:] = x
    for move in moves:
        move.wait()
    out_rows = solved.shape[0]
    solved_copy = pltpu.make_async_copy(
        xs.at[pl.ds(pl.multiple_of(position * out_rows, out_rows), out_rows)], solved, sems.at[0]
    )
    solved_copy.start()
    update = jnp.dot(masked[:, last:], x, preferred_element_type=jnp.float32)
    out[...] = (total[...] - update).astype(jnp.bfloat16)
    updated_copy = pltpu.make_async_copy(out, updated, sems.at[1])
    updated_copy.start()
    solved_copy.wait()
    updated_copy.wait()


def last(inverse, far, masked, segments, start, solutions, total, n_row):
    rows, columns = total.shape
    return pl.pallas_call(
        last_kernel,
        out_shape=(
            jax.ShapeDtypeStruct((SN * SNR // n_row, columns), jnp.bfloat16),
            jax.ShapeDtypeStruct((rows, columns), jnp.bfloat16),
        ),
        in_specs=[VMEM] * 7,
        out_specs=(ANY, ANY),
        scratch_shapes=[
            pltpu.VMEM((SN * SNR, columns), jnp.bfloat16),
            pltpu.VMEM((rows, columns), jnp.bfloat16),
            pltpu.SemaphoreType.DMA((2,)),
        ],
        compiler_params=PARAMS,
        name="last",
    )(inverse, far, masked, segments, start, solutions, total)


def on_device(right_side, factor, pattern, inverses, owners, offsets):
    n_row, n_src = lax.axis_size("row"), lax.axis_size("src")
    piece, segment = stage(owners, offsets, pattern, factor, right_side, n_src)
    pieces = line_gather(piece, n_row)
    inverse = join(src_gather(inverses, n_src))
    near, far = pick(owners, pieces, n_row)
    near, far, inverse = lax.optimization_barrier((near, far, inverse))
    near, far = join(src_gather(near, n_src)), join(src_gather(far, n_src))
    masked = mask(owners, offsets, pattern, factor)
    slots = line_gather(segment, n_row)
    segments, start, total = first(owners, inverse, masked, right_side, slots, n_row)
    solutions, total = middle(inverse, near, masked, segments, start, total)
    return last(inverse, far, masked, segments, start, solutions, total, n_row)


def solution(mesh):
    placed = (
        P(("group", "row"), "src"),
        P(("group", "row"), None),
        P(("group", "row"), None),
        P("group", "src", None),
        P("group"),
        P("group"),
    )
    return jax.shard_map(
        on_device,
        mesh=mesh,
        in_specs=placed,
        out_specs=(P(("group", "row"), "src"), P(("group", "row"), "src")),
        check_vma=False,
    )
```

```python
import functools

import jax
import jax.numpy as jnp
from jax import lax
from jax.experimental import pallas as pl
from jax.experimental.pallas import tpu as pltpu
from jax.sharding import PartitionSpec as P

SN = 4
SNR = 512
BLK = 128
LEFT = (SN - 1) * SNR
ANY = pl.BlockSpec(memory_space=pl.ANY)
SMEM = pl.BlockSpec(memory_space=pltpu.SMEM)
VMEM = pl.BlockSpec(memory_space=pltpu.VMEM)
PARAMS = pltpu.CompilerParams(vmem_limit_bytes=24 << 20)


def line_gather(value, n):
    slots = [value]
    for chain in range(2):
        got = value
        for hop in range(1, n):
            pairs = []
            for i in range(n):
                side = 1 if (i + chain + hop) % 2 else -1
                there, back = i + side * hop, i - side * (hop - 1)
                if 0 <= i + side < n and (0 <= there < n or 0 <= back < n):
                    pairs.append((i + side, i))
            got = lax.ppermute(got, "row", pairs) if pairs else None
            slots.append(got)
    return slots


def slot_of(owner, n):
    position = lax.axis_index("row")
    away = owner - position
    hop = jnp.abs(away)
    side = jnp.where(away > 0, 1, 0)
    chain = lax.rem(position + hop + side, 2)
    return jnp.where(away == 0, 0, hop + chain * (n - 1))


def src_gather(value, n):
    pieces = {0: value}
    bit = n // 2
    while bit:
        for distance in list(pieces):
            pieces[distance ^ bit] = lax.ppermute(
                pieces[distance], "src", [(i, i ^ bit) for i in range(n)]
            )
        bit //= 2
    return [pieces[d] for d in range(n)]


def own_start(owners, offsets):
    position = lax.axis_index("row")
    start = jnp.int32(0)
    for node in range(SN):
        start = jnp.where(owners[node] == position, offsets[node] * BLK, start)
    return start


def start_matching(slots, wanted, place):
    for index, slot in enumerate(slots):
        if slot is not None:

            @pl.when(wanted == index)
            def _(slot=slot):
                place(slot).start()


def fill(held, refs):
    refs = iter(refs)
    return [next(refs) if there else None for there in held]


def stage_kernel(quarter, owners, offsets, pattern, factor, right, piece, segment, rows, sems):
    start = pl.multiple_of(own_start(owners, offsets), BLK)
    first = pl.multiple_of(start + lax.axis_index("src") * quarter, quarter)
    fetch = pltpu.make_async_copy(factor.at[pl.ds(first, quarter), pl.ds(0, LEFT)], rows, sems.at[0])
    move = pltpu.make_async_copy(right.at[pl.ds(start, SNR)], segment, sems.at[1])
    fetch.start()
    move.start()
    fetch.wait()
    tall = min(quarter, BLK)
    for top in range(0, quarter, tall):
        tile_row = (first + top) // BLK
        for col in range(0, LEFT, BLK):
            tile = rows[top : top + tall, col : col + BLK]
            kept = jnp.where(pattern[tile_row, col // BLK] > 0, tile, jnp.zeros_like(tile))
            piece[top : top + tall, col : col + BLK] = kept
    move.wait()


def stage(owners, offsets, pattern, factor, right, n_src):
    quarter = SNR // n_src
    shapes = [(quarter, LEFT), (SNR, right.shape[1])]
    return pl.pallas_call(
        functools.partial(stage_kernel, quarter),
        out_shape=[jax.ShapeDtypeStruct(shape, jnp.bfloat16) for shape in shapes],
        in_specs=[SMEM] * 3 + [ANY] * 2,
        out_specs=[VMEM, VMEM],
        scratch_shapes=[
            pltpu.VMEM((quarter, LEFT), jnp.bfloat16),
            pltpu.SemaphoreType.DMA((2,)),
        ],
        compiler_params=pltpu.CompilerParams(vmem_limit_bytes=56 << 20),
        name="stage",
    )(owners, offsets, pattern, factor, right)


def pick_kernel(n_row, held, owners, *refs):
    slots = fill(held, refs[: sum(held)])
    near, far, sems = refs[sum(held) :]

    def place(node, slot):
        width = node * SNR
        first = 0 if node == SN - 1 else node * (node - 1) // 2 * SNR
        target = (far if node == SN - 1 else near).at[:, pl.ds(first, width)]
        return pltpu.make_async_copy(slot.at[:, pl.ds(0, width)], target, sems.at[node])

    for node in range(1, SN):
        start_matching(slots, slot_of(owners[node], n_row), functools.partial(place, node))
    for node in range(1, SN):
        place(node, slots[0]).wait()


def pick(owners, slots, n_row):
    held = [slot is not None for slot in slots]
    quarter = slots[0].shape[0]
    shapes = [(quarter, (SN - 1) * (SN - 2) // 2 * SNR), (quarter, LEFT)]
    return pl.pallas_call(
        functools.partial(pick_kernel, n_row, held),
        out_shape=[jax.ShapeDtypeStruct(shape, jnp.bfloat16) for shape in shapes],
        in_specs=[SMEM] + [ANY] * sum(held),
        out_specs=[ANY] * 2,
        scratch_shapes=[pltpu.SemaphoreType.DMA((SN,))],
        compiler_params=PARAMS,
        name="pick",
    )(owners, *(slot for slot in slots if slot is not None))


def join_copies(pieces, whole, sems, cols=None):
    me, quarter = lax.axis_index("src"), SNR // len(pieces)
    copies = []
    for d, piece in enumerate(pieces):
        rows = pl.ds(pl.multiple_of(jnp.bitwise_xor(me, d) * quarter, quarter), quarter)
        place = whole.at[rows] if len(whole.shape) == 2 else whole.at[:, rows]
        if cols is not None:
            piece, place = piece.at[:, cols], whole.at[rows, cols]
        copies.append(pltpu.make_async_copy(piece, place, sems.at[d]))
    return copies


def join_kernel(*refs):
    *pieces, whole, sems = refs
    copies = join_copies(pieces, whole, sems)
    for copy in copies:
        copy.start()
    for copy in copies:
        copy.wait()


def join(pieces):
    shape = pieces[0].shape[:-2] + (SNR, pieces[0].shape[-1])
    return pl.pallas_call(
        join_kernel,
        out_shape=jax.ShapeDtypeStruct(shape, jnp.bfloat16),
        in_specs=[ANY] * len(pieces),
        out_specs=ANY,
        scratch_shapes=[pltpu.SemaphoreType.DMA((len(pieces),))],
        compiler_params=PARAMS,
        name="join",
    )(*pieces)


def mask_kernel(owners, offsets, pattern, factor, masked):
    start = own_start(owners, offsets)
    position = lax.axis_index("row")
    owned = jnp.int32(SN)
    for node in range(SN):
        owned = jnp.where(owners[node] == position, node, owned)
    for top in range(0, factor.shape[0], BLK):
        rank = jnp.where((top >= start) & (top < start + SNR), owned, SN)
        for col in range(0, factor.shape[1], BLK):
            keep = (pattern[top // BLK, col // BLK] > 0) & (rank > col // SNR)
            tile = factor[top : top + BLK, col : col + BLK]
            masked[top : top + BLK, col : col + BLK] = jnp.where(keep, tile, jnp.zeros_like(tile))


def mask(owners, offsets, pattern, factor):
    return pl.pallas_call(
        mask_kernel,
        out_shape=jax.ShapeDtypeStruct(factor.shape, factor.dtype),
        in_specs=[SMEM] * 3 + [pl.BlockSpec(memory_space=pltpu.VMEM)],
        out_specs=pl.BlockSpec(memory_space=pltpu.VMEM),
        compiler_params=PARAMS,
        name="mask",
    )(owners, offsets, pattern, factor)


def first_kernel(n_row, held, owners, inverse, masked, right, *refs):
    slots = fill(held, refs[: sum(held)])
    segments, solution, total, segment, sems = refs[sum(held) :]

    def place(node, slot):
        target = segments.at[node - 1] if node else segment
        return pltpu.make_async_copy(slot, target, sems.at[node])

    for node in range(SN):
        start_matching(slots, slot_of(owners[node], n_row), functools.partial(place, node))
    place(0, slots[0]).wait()
    x = jnp.dot(inverse[0], segment[...], preferred_element_type=jnp.float32).astype(jnp.bfloat16)
    solution[...] = x
    update = jnp.dot(masked[:, :SNR], x, preferred_element_type=jnp.float32)
    total[...] = right[...].astype(jnp.float32) - update
    for node in range(1, SN):
        place(node, slots[0]).wait()


def first(owners, inverse, masked, right, slots, n_row):
    held = [slot is not None for slot in slots]
    rows, columns = right.shape
    return pl.pallas_call(
        functools.partial(first_kernel, n_row, held),
        out_shape=(
            jax.ShapeDtypeStruct((SN - 1, SNR, columns), jnp.bfloat16),
            jax.ShapeDtypeStruct((SNR, columns), jnp.bfloat16),
            jax.ShapeDtypeStruct((rows, columns), jnp.float32),
        ),
        in_specs=[SMEM] + [VMEM] * 3 + [ANY] * sum(held),
        out_specs=(ANY, VMEM, VMEM),
        scratch_shapes=[
            pltpu.VMEM((SNR, columns), jnp.bfloat16),
            pltpu.SemaphoreType.DMA((SN,)),
        ],
        compiler_params=PARAMS,
        cost_estimate=pl.CostEstimate(flops=60 * 10**9, bytes_accessed=0, transcendentals=0),
        name="first",
    )(owners, inverse, masked, right, *(slot for slot in slots if slot is not None))


def middle_kernel(inverse, masked, segments, start, before, *refs):
    *pieces, solutions, total, near, sems = refs
    copies = {
        node: join_copies(
            pieces, near, sems.at[node - 1], pl.ds(node * (node - 1) // 2 * SNR, node * SNR)
        )
        for node in range(1, SN - 1)
    }
    for node in copies:
        for copy in copies[node]:
            copy.start()
    left = before[...]
    for node in range(1, SN - 1):
        for copy in copies[node]:
            copy.wait()
        at = node * (node - 1) // 2 * SNR
        update = jnp.dot(near[:, at : at + SNR], start[...], preferred_element_type=jnp.float32)
        if node > 1:
            update += jnp.dot(
                near[:, at + SNR : at + node * SNR],
                solutions[: (node - 1) * SNR],
                preferred_element_type=jnp.float32,
            )
        segment = (segments[node - 1].astype(jnp.float32) - update).astype(jnp.bfloat16)
        x = jnp.dot(inverse[node], segment, preferred_element_type=jnp.float32).astype(jnp.bfloat16)
        solutions[(node - 1) * SNR : node * SNR] = x
    cols = masked[:, SNR : (SN - 1) * SNR]
    total[...] = left - jnp.dot(cols, solutions[...], preferred_element_type=jnp.float32)


def middle(inverse, near, masked, segments, start, total):
    columns = start.shape[1]
    return pl.pallas_call(
        middle_kernel,
        out_shape=(
            jax.ShapeDtypeStruct(((SN - 2) * SNR, columns), jnp.bfloat16),
            jax.ShapeDtypeStruct(total.shape, jnp.float32),
        ),
        in_specs=[VMEM] * 5 + [ANY] * len(near),
        out_specs=(VMEM, VMEM),
        scratch_shapes=[pltpu.VMEM((SNR, near[0].shape[1]), jnp.bfloat16), pltpu.SemaphoreType.DMA((SN - 2, len(near)))],
        compiler_params=PARAMS,
        cost_estimate=pl.CostEstimate(flops=24 * 10**9, bytes_accessed=0, transcendentals=0),
        name="middle",
    )(inverse, masked, segments, start, total, *near)


def last_kernel(inverse, masked, segments, start, solutions, total, *refs):
    *pieces, solved, updated, far, xs, out, sems, far_sems = refs
    copies = [
        join_copies(pieces, far, far_sems.at[i], cols)
        for i, cols in enumerate((pl.ds(0, SNR), pl.ds(SNR, LEFT - SNR)))
    ]
    for copy in copies[0] + copies[1]:
        copy.start()
    position = lax.axis_index("row")
    last = (SN - 1) * SNR
    moves = [
        pltpu.make_async_copy(start, xs.at[pl.ds(0, SNR)], sems.at[0]),
        pltpu.make_async_copy(solutions, xs.at[pl.ds(SNR, last - SNR)], sems.at[1]),
    ]
    for move in moves:
        move.start()
    for copy in copies[0]:
        copy.wait()
    update = jnp.dot(far[:, :SNR], start[...], preferred_element_type=jnp.float32)
    for copy in copies[1]:
        copy.wait()
    update += jnp.dot(far[:, SNR:], solutions[...], preferred_element_type=jnp.float32)
    segment = (segments[SN - 2].astype(jnp.float32) - update).astype(jnp.bfloat16)
    x = jnp.dot(inverse[SN - 1], segment, preferred_element_type=jnp.float32).astype(jnp.bfloat16)
    xs[last:] = x
    for move in moves:
        move.wait()
    out_rows = solved.shape[0]
    solved_copy = pltpu.make_async_copy(
        xs.at[pl.ds(pl.multiple_of(position * out_rows, out_rows), out_rows)], solved, sems.at[0]
    )
    solved_copy.start()
    update = jnp.dot(masked[:, last:], x, preferred_element_type=jnp.float32)
    out[...] = (total[...] - update).astype(jnp.bfloat16)
    updated_copy = pltpu.make_async_copy(out, updated, sems.at[1])
    updated_copy.start()
    solved_copy.wait()
    updated_copy.wait()


def last(inverse, far, masked, segments, start, solutions, total, n_row):
    rows, columns = total.shape
    return pl.pallas_call(
        last_kernel,
        out_shape=(
            jax.ShapeDtypeStruct((SN * SNR // n_row, columns), jnp.bfloat16),
            jax.ShapeDtypeStruct((rows, columns), jnp.bfloat16),
        ),
        in_specs=[VMEM] * 6 + [ANY] * len(far),
        out_specs=(ANY, ANY),
        scratch_shapes=[
            pltpu.VMEM((SNR, LEFT), jnp.bfloat16),
            pltpu.VMEM((SN * SNR, columns), jnp.bfloat16),
            pltpu.VMEM((rows, columns), jnp.bfloat16),
            pltpu.SemaphoreType.DMA((2,)),
            pltpu.SemaphoreType.DMA((2, len(far))),
        ],
        compiler_params=PARAMS,
        name="last",
    )(inverse, masked, segments, start, solutions, total, *far)


def on_device(right_side, factor, pattern, inverses, owners, offsets):
    n_row, n_src = lax.axis_size("row"), lax.axis_size("src")
    piece, segment = stage(owners, offsets, pattern, factor, right_side, n_src)
    pieces = line_gather(piece, n_row)
    inverse = join(src_gather(inverses, n_src))
    near, far = pick(owners, pieces, n_row)
    near, far, inverse = lax.optimization_barrier((near, far, inverse))
    near, far = src_gather(near, n_src), src_gather(far, n_src)
    masked = mask(owners, offsets, pattern, factor)
    slots = line_gather(segment, n_row)
    segments, start, total = first(owners, inverse, masked, right_side, slots, n_row)
    solutions, total = middle(inverse, near, masked, segments, start, total)
    return last(inverse, far, masked, segments, start, solutions, total, n_row)


def solution(mesh):
    placed = (
        P(("group", "row"), "src"),
        P(("group", "row"), None),
        P(("group", "row"), None),
        P("group", "src", None),
        P("group"),
        P("group"),
    )
    return jax.shard_map(
        on_device,
        mesh=mesh,
        in_specs=placed,
        out_specs=(P(("group", "row"), "src"), P(("group", "row"), "src")),
        check_vma=False,
    )
```

```python
import functools

import jax
import jax.numpy as jnp
from jax import lax
from jax.experimental import pallas as pl
from jax.experimental.pallas import tpu as pltpu
from jax.sharding import PartitionSpec as P

SN = 4
SNR = 512
BLK = 128
LEFT = (SN - 1) * SNR
ANY = pl.BlockSpec(memory_space=pl.ANY)
SMEM = pl.BlockSpec(memory_space=pltpu.SMEM)
VMEM = pl.BlockSpec(memory_space=pltpu.VMEM)
PARAMS = pltpu.CompilerParams(vmem_limit_bytes=24 << 20)


def line_gather(value, n):
    slots = [value]
    for chain in range(2):
        got = value
        for hop in range(1, n):
            pairs = []
            for i in range(n):
                side = 1 if (i + chain + hop) % 2 else -1
                there, back = i + side * hop, i - side * (hop - 1)
                if 0 <= i + side < n and (0 <= there < n or 0 <= back < n):
                    pairs.append((i + side, i))
            got = lax.ppermute(got, "row", pairs) if pairs else None
            slots.append(got)
    return slots


def slot_of(owner, n):
    position = lax.axis_index("row")
    away = owner - position
    hop = jnp.abs(away)
    side = jnp.where(away > 0, 1, 0)
    chain = lax.rem(position + hop + side, 2)
    return jnp.where(away == 0, 0, hop + chain * (n - 1))


def src_gather(value, n):
    pieces = {0: value}
    bit = n // 2
    while bit:
        for distance in list(pieces):
            pieces[distance ^ bit] = lax.ppermute(
                pieces[distance], "src", [(i, i ^ bit) for i in range(n)]
            )
        bit //= 2
    return [pieces[d] for d in range(n)]


def own_start(owners, offsets):
    position = lax.axis_index("row")
    start = jnp.int32(0)
    for node in range(SN):
        start = jnp.where(owners[node] == position, offsets[node] * BLK, start)
    return start


def start_matching(slots, wanted, place):
    for index, slot in enumerate(slots):
        if slot is not None:

            @pl.when(wanted == index)
            def _(slot=slot):
                place(slot).start()


def fill(held, refs):
    refs = iter(refs)
    return [next(refs) if there else None for there in held]


def stage_kernel(quarter, owners, offsets, pattern, factor, right, piece, segment, sems):
    start = pl.multiple_of(own_start(owners, offsets), BLK)
    first = pl.multiple_of(start + lax.axis_index("src") * quarter, quarter)
    fetch = pltpu.make_async_copy(
        factor.at[pl.ds(first, quarter), pl.ds(0, LEFT)], piece, sems.at[0]
    )
    move = pltpu.make_async_copy(right.at[pl.ds(start, SNR)], segment, sems.at[1])
    fetch.start()
    move.start()
    fetch.wait()
    tall = min(quarter, BLK)
    for top in range(0, quarter, tall):
        tile_row = (first + top) // BLK
        for col in range(0, LEFT, BLK):

            @pl.when(pattern[tile_row, col // BLK] <= 0)
            def _(top=top, col=col):
                piece[top : top + tall, col : col + BLK] = jnp.zeros((tall, BLK), piece.dtype)

    move.wait()


def stage(owners, offsets, pattern, factor, right, n_src):
    quarter = SNR // n_src
    shapes = [(quarter, LEFT), (SNR, right.shape[1])]
    return pl.pallas_call(
        functools.partial(stage_kernel, quarter),
        out_shape=[jax.ShapeDtypeStruct(shape, jnp.bfloat16) for shape in shapes],
        in_specs=[SMEM] * 3 + [ANY] * 2,
        out_specs=[VMEM, VMEM],
        scratch_shapes=[pltpu.SemaphoreType.DMA((2,))],
        compiler_params=pltpu.CompilerParams(vmem_limit_bytes=56 << 20),
        name="stage",
    )(owners, offsets, pattern, factor, right)


def pick_kernel(n_row, held, owners, *refs):
    slots = fill(held, refs[: sum(held)])
    near, far, sems = refs[sum(held) :]

    def place(node, slot):
        width = node * SNR
        first = 0 if node == SN - 1 else node * (node - 1) // 2 * SNR
        target = (far if node == SN - 1 else near).at[:, pl.ds(first, width)]
        return pltpu.make_async_copy(slot.at[:, pl.ds(0, width)], target, sems.at[node])

    for node in range(1, SN):
        start_matching(slots, slot_of(owners[node], n_row), functools.partial(place, node))
    for node in range(1, SN):
        place(node, slots[0]).wait()


def pick(owners, slots, n_row):
    held = [slot is not None for slot in slots]
    quarter = slots[0].shape[0]
    shapes = [(quarter, (SN - 1) * (SN - 2) // 2 * SNR), (quarter, LEFT)]
    return pl.pallas_call(
        functools.partial(pick_kernel, n_row, held),
        out_shape=[jax.ShapeDtypeStruct(shape, jnp.bfloat16) for shape in shapes],
        in_specs=[SMEM] + [ANY] * sum(held),
        out_specs=[ANY] * 2,
        scratch_shapes=[pltpu.SemaphoreType.DMA((SN,))],
        compiler_params=PARAMS,
        name="pick",
    )(owners, *(slot for slot in slots if slot is not None))


def join_copies(pieces, whole, sems, cols=None):
    me, quarter = lax.axis_index("src"), SNR // len(pieces)
    copies = []
    for d, piece in enumerate(pieces):
        rows = pl.ds(pl.multiple_of(jnp.bitwise_xor(me, d) * quarter, quarter), quarter)
        place = whole.at[rows] if len(whole.shape) == 2 else whole.at[:, rows]
        if cols is not None:
            piece, place = piece.at[:, cols], whole.at[rows, cols]
        copies.append(pltpu.make_async_copy(piece, place, sems.at[d]))
    return copies


def join_kernel(*refs):
    *pieces, whole, sems = refs
    copies = join_copies(pieces, whole, sems)
    for copy in copies:
        copy.start()
    for copy in copies:
        copy.wait()


def join(pieces):
    shape = pieces[0].shape[:-2] + (SNR, pieces[0].shape[-1])
    return pl.pallas_call(
        join_kernel,
        out_shape=jax.ShapeDtypeStruct(shape, jnp.bfloat16),
        in_specs=[ANY] * len(pieces),
        out_specs=ANY,
        scratch_shapes=[pltpu.SemaphoreType.DMA((len(pieces),))],
        compiler_params=PARAMS,
        name="join",
    )(*pieces)


def mask_kernel(owners, offsets, pattern, factor, masked):
    start = own_start(owners, offsets)
    position = lax.axis_index("row")
    owned = jnp.int32(SN)
    for node in range(SN):
        owned = jnp.where(owners[node] == position, node, owned)
    for top in range(0, factor.shape[0], BLK):
        rank = jnp.where((top >= start) & (top < start + SNR), owned, SN)
        for col in range(0, factor.shape[1], BLK):
            keep = (pattern[top // BLK, col // BLK] > 0) & (rank > col // SNR)
            tile = factor[top : top + BLK, col : col + BLK]
            masked[top : top + BLK, col : col + BLK] = jnp.where(keep, tile, jnp.zeros_like(tile))


def mask(owners, offsets, pattern, factor):
    return pl.pallas_call(
        mask_kernel,
        out_shape=jax.ShapeDtypeStruct(factor.shape, factor.dtype),
        in_specs=[SMEM] * 3 + [pl.BlockSpec(memory_space=pltpu.VMEM)],
        out_specs=pl.BlockSpec(memory_space=pltpu.VMEM),
        compiler_params=PARAMS,
        name="mask",
    )(owners, offsets, pattern, factor)


def first_kernel(n_row, held, owners, inverse, masked, right, *refs):
    slots = fill(held, refs[: sum(held)])
    segments, solution, total, segment, sems = refs[sum(held) :]

    def place(node, slot):
        target = segments.at[node - 1] if node else segment
        return pltpu.make_async_copy(slot, target, sems.at[node])

    for node in range(SN):
        start_matching(slots, slot_of(owners[node], n_row), functools.partial(place, node))
    place(0, slots[0]).wait()
    x = jnp.dot(inverse[0], segment[...], preferred_element_type=jnp.float32).astype(jnp.bfloat16)
    solution[...] = x
    update = jnp.dot(masked[:, :SNR], x, preferred_element_type=jnp.float32)
    total[...] = right[...].astype(jnp.float32) - update
    for node in range(1, SN):
        place(node, slots[0]).wait()


def first(owners, inverse, masked, right, slots, n_row):
    held = [slot is not None for slot in slots]
    rows, columns = right.shape
    return pl.pallas_call(
        functools.partial(first_kernel, n_row, held),
        out_shape=(
            jax.ShapeDtypeStruct((SN - 1, SNR, columns), jnp.bfloat16),
            jax.ShapeDtypeStruct((SNR, columns), jnp.bfloat16),
            jax.ShapeDtypeStruct((rows, columns), jnp.float32),
        ),
        in_specs=[SMEM] + [VMEM] * 3 + [ANY] * sum(held),
        out_specs=(ANY, VMEM, VMEM),
        scratch_shapes=[
            pltpu.VMEM((SNR, columns), jnp.bfloat16),
            pltpu.SemaphoreType.DMA((SN,)),
        ],
        compiler_params=PARAMS,
        cost_estimate=pl.CostEstimate(flops=60 * 10**9, bytes_accessed=0, transcendentals=0),
        name="first",
    )(owners, inverse, masked, right, *(slot for slot in slots if slot is not None))


def middle_kernel(inverse, masked, segments, start, before, *refs):
    *pieces, solutions, total, near, sems = refs
    copies = {
        node: join_copies(
            pieces, near, sems.at[node - 1], pl.ds(node * (node - 1) // 2 * SNR, node * SNR)
        )
        for node in range(1, SN - 1)
    }
    for node in copies:
        for copy in copies[node]:
            copy.start()
    left = before[...]
    for node in range(1, SN - 1):
        for copy in copies[node]:
            copy.wait()
        at = node * (node - 1) // 2 * SNR
        update = jnp.dot(near[:, at : at + SNR], start[...], preferred_element_type=jnp.float32)
        if node > 1:
            update += jnp.dot(
                near[:, at + SNR : at + node * SNR],
                solutions[: (node - 1) * SNR],
                preferred_element_type=jnp.float32,
            )
        segment = (segments[node - 1].astype(jnp.float32) - update).astype(jnp.bfloat16)
        x = jnp.dot(inverse[node], segment, preferred_element_type=jnp.float32).astype(jnp.bfloat16)
        solutions[(node - 1) * SNR : node * SNR] = x
    cols = masked[:, SNR : (SN - 1) * SNR]
    total[...] = left - jnp.dot(cols, solutions[...], preferred_element_type=jnp.float32)


def middle(inverse, near, masked, segments, start, total):
    columns = start.shape[1]
    return pl.pallas_call(
        middle_kernel,
        out_shape=(
            jax.ShapeDtypeStruct(((SN - 2) * SNR, columns), jnp.bfloat16),
            jax.ShapeDtypeStruct(total.shape, jnp.float32),
        ),
        in_specs=[VMEM] * 5 + [ANY] * len(near),
        out_specs=(VMEM, VMEM),
        scratch_shapes=[pltpu.VMEM((SNR, near[0].shape[1]), jnp.bfloat16), pltpu.SemaphoreType.DMA((SN - 2, len(near)))],
        compiler_params=PARAMS,
        cost_estimate=pl.CostEstimate(flops=24 * 10**9, bytes_accessed=0, transcendentals=0),
        name="middle",
    )(inverse, masked, segments, start, total, *near)


def last_kernel(inverse, masked, segments, start, solutions, total, *refs):
    *pieces, solved, updated, far, xs, out, sems, far_sems = refs
    copies = [
        join_copies(pieces, far, far_sems.at[i], cols)
        for i, cols in enumerate((pl.ds(0, SNR), pl.ds(SNR, LEFT - SNR)))
    ]
    for copy in copies[0] + copies[1]:
        copy.start()
    position = lax.axis_index("row")
    last = (SN - 1) * SNR
    moves = [
        pltpu.make_async_copy(start, xs.at[pl.ds(0, SNR)], sems.at[0]),
        pltpu.make_async_copy(solutions, xs.at[pl.ds(SNR, last - SNR)], sems.at[1]),
    ]
    for move in moves:
        move.start()
    for copy in copies[0]:
        copy.wait()
    update = jnp.dot(far[:, :SNR], start[...], preferred_element_type=jnp.float32)
    for copy in copies[1]:
        copy.wait()
    update += jnp.dot(far[:, SNR:], solutions[...], preferred_element_type=jnp.float32)
    segment = (segments[SN - 2].astype(jnp.float32) - update).astype(jnp.bfloat16)
    x = jnp.dot(inverse[SN - 1], segment, preferred_element_type=jnp.float32).astype(jnp.bfloat16)
    xs[last:] = x
    for move in moves:
        move.wait()
    out_rows = solved.shape[0]
    solved_copy = pltpu.make_async_copy(
        xs.at[pl.ds(pl.multiple_of(position * out_rows, out_rows), out_rows)], solved, sems.at[0]
    )
    solved_copy.start()
    update = jnp.dot(masked[:, last:], x, preferred_element_type=jnp.float32)
    out[...] = (total[...] - update).astype(jnp.bfloat16)
    updated_copy = pltpu.make_async_copy(out, updated, sems.at[1])
    updated_copy.start()
    solved_copy.wait()
    updated_copy.wait()


def last(inverse, far, masked, segments, start, solutions, total, n_row):
    rows, columns = total.shape
    return pl.pallas_call(
        last_kernel,
        out_shape=(
            jax.ShapeDtypeStruct((SN * SNR // n_row, columns), jnp.bfloat16),
            jax.ShapeDtypeStruct((rows, columns), jnp.bfloat16),
        ),
        in_specs=[VMEM] * 6 + [ANY] * len(far),
        out_specs=(ANY, ANY),
        scratch_shapes=[
            pltpu.VMEM((SNR, LEFT), jnp.bfloat16),
            pltpu.VMEM((SN * SNR, columns), jnp.bfloat16),
            pltpu.VMEM((rows, columns), jnp.bfloat16),
            pltpu.SemaphoreType.DMA((2,)),
            pltpu.SemaphoreType.DMA((2, len(far))),
        ],
        compiler_params=PARAMS,
        name="last",
    )(inverse, masked, segments, start, solutions, total, *far)


def on_device(right_side, factor, pattern, inverses, owners, offsets):
    n_row, n_src = lax.axis_size("row"), lax.axis_size("src")
    piece, segment = stage(owners, offsets, pattern, factor, right_side, n_src)
    pieces = line_gather(piece, n_row)
    inverse = join(src_gather(inverses, n_src))
    near, far = pick(owners, pieces, n_row)
    near, far, inverse = lax.optimization_barrier((near, far, inverse))
    near, far = src_gather(near, n_src), src_gather(far, n_src)
    masked = mask(owners, offsets, pattern, factor)
    slots = line_gather(segment, n_row)
    segments, start, total = first(owners, inverse, masked, right_side, slots, n_row)
    solutions, total = middle(inverse, near, masked, segments, start, total)
    return last(inverse, far, masked, segments, start, solutions, total, n_row)


def solution(mesh):
    placed = (
        P(("group", "row"), "src"),
        P(("group", "row"), None),
        P(("group", "row"), None),
        P("group", "src", None),
        P("group"),
        P("group"),
    )
    return jax.shard_map(
        on_device,
        mesh=mesh,
        in_specs=placed,
        out_specs=(P(("group", "row"), "src"), P(("group", "row"), "src")),
        check_vma=False,
    )
```

```python
import functools

import jax
import jax.numpy as jnp
from jax import lax
from jax.experimental import pallas as pl
from jax.experimental.pallas import tpu as pltpu
from jax.sharding import PartitionSpec as P

SN = 4
SNR = 512
BLK = 128
LEFT = (SN - 1) * SNR
ANY = pl.BlockSpec(memory_space=pl.ANY)
SMEM = pl.BlockSpec(memory_space=pltpu.SMEM)
VMEM = pl.BlockSpec(memory_space=pltpu.VMEM)
PARAMS = pltpu.CompilerParams(vmem_limit_bytes=24 << 20)


def line_gather(value, n):
    slots = [value]
    for chain in range(2):
        got = value
        for hop in range(1, n):
            pairs = []
            for i in range(n):
                side = 1 if (i + chain + hop) % 2 else -1
                there, back = i + side * hop, i - side * (hop - 1)
                if 0 <= i + side < n and (0 <= there < n or 0 <= back < n):
                    pairs.append((i + side, i))
            got = lax.ppermute(got, "row", pairs) if pairs else None
            slots.append(got)
    return slots


def slot_of(owner, n):
    position = lax.axis_index("row")
    away = owner - position
    hop = jnp.abs(away)
    side = jnp.where(away > 0, 1, 0)
    chain = lax.rem(position + hop + side, 2)
    return jnp.where(away == 0, 0, hop + chain * (n - 1))


def src_gather(value, n):
    pieces = {0: value}
    bit = n // 2
    while bit:
        for distance in list(pieces):
            pieces[distance ^ bit] = lax.ppermute(
                pieces[distance], "src", [(i, i ^ bit) for i in range(n)]
            )
        bit //= 2
    return [pieces[d] for d in range(n)]


def own_start(owners, offsets):
    position = lax.axis_index("row")
    start = jnp.int32(0)
    for node in range(SN):
        start = jnp.where(owners[node] == position, offsets[node] * BLK, start)
    return start


def start_matching(slots, wanted, place):
    for index, slot in enumerate(slots):
        if slot is not None:

            @pl.when(wanted == index)
            def _(slot=slot):
                place(slot).start()


def fill(held, refs):
    refs = iter(refs)
    return [next(refs) if there else None for there in held]


def stage_kernel(quarter, owners, offsets, pattern, factor, right, piece, segment, sems):
    start = pl.multiple_of(own_start(owners, offsets), BLK)
    first = pl.multiple_of(start + lax.axis_index("src") * quarter, quarter)
    fetch = pltpu.make_async_copy(
        factor.at[pl.ds(first, quarter), pl.ds(0, LEFT)], piece, sems.at[0]
    )
    move = pltpu.make_async_copy(right.at[pl.ds(start, SNR)], segment, sems.at[1])
    fetch.start()
    move.start()
    fetch.wait()
    tall = min(quarter, BLK)
    for top in range(0, quarter, tall):
        tile_row = (first + top) // BLK
        for col in range(0, LEFT, BLK):

            @pl.when(pattern[tile_row, col // BLK] <= 0)
            def _(top=top, col=col):
                piece[top : top + tall, col : col + BLK] = jnp.zeros((tall, BLK), piece.dtype)

    move.wait()


def stage(owners, offsets, pattern, factor, right, n_src):
    quarter = SNR // n_src
    shapes = [(quarter, LEFT), (SNR, right.shape[1])]
    return pl.pallas_call(
        functools.partial(stage_kernel, quarter),
        out_shape=[jax.ShapeDtypeStruct(shape, jnp.bfloat16) for shape in shapes],
        in_specs=[SMEM] * 3 + [ANY] * 2,
        out_specs=[VMEM, VMEM],
        scratch_shapes=[pltpu.SemaphoreType.DMA((2,))],
        compiler_params=pltpu.CompilerParams(vmem_limit_bytes=56 << 20),
        name="stage",
    )(owners, offsets, pattern, factor, right)


def pick_kernel(n_row, held, owners, *refs):
    slots = fill(held, refs[: sum(held)])
    near, far, sems = refs[sum(held) :]

    def place(node, slot):
        width = node * SNR
        first = 0 if node == SN - 1 else node * (node - 1) // 2 * SNR
        target = (far if node == SN - 1 else near).at[:, pl.ds(first, width)]
        return pltpu.make_async_copy(slot.at[:, pl.ds(0, width)], target, sems.at[node])

    for node in range(1, SN):
        start_matching(slots, slot_of(owners[node], n_row), functools.partial(place, node))
    for node in range(1, SN):
        place(node, slots[0]).wait()


def pick(owners, slots, n_row):
    held = [slot is not None for slot in slots]
    quarter = slots[0].shape[0]
    shapes = [(quarter, (SN - 1) * (SN - 2) // 2 * SNR), (quarter, LEFT)]
    return pl.pallas_call(
        functools.partial(pick_kernel, n_row, held),
        out_shape=[jax.ShapeDtypeStruct(shape, jnp.bfloat16) for shape in shapes],
        in_specs=[SMEM] + [ANY] * sum(held),
        out_specs=[ANY] * 2,
        scratch_shapes=[pltpu.SemaphoreType.DMA((SN,))],
        compiler_params=PARAMS,
        name="pick",
    )(owners, *(slot for slot in slots if slot is not None))


def join_copies(pieces, whole, sems, cols=None):
    me, quarter = lax.axis_index("src"), SNR // len(pieces)
    copies = []
    for d, piece in enumerate(pieces):
        rows = pl.ds(pl.multiple_of(jnp.bitwise_xor(me, d) * quarter, quarter), quarter)
        place = whole.at[rows] if len(whole.shape) == 2 else whole.at[:, rows]
        if cols is not None:
            piece, place = piece.at[:, cols], whole.at[rows, cols]
        copies.append(pltpu.make_async_copy(piece, place, sems.at[d]))
    return copies


def join_kernel(*refs):
    *pieces, whole, sems = refs
    copies = join_copies(pieces, whole, sems)
    for copy in copies:
        copy.start()
    for copy in copies:
        copy.wait()


def join(pieces):
    shape = pieces[0].shape[:-2] + (SNR, pieces[0].shape[-1])
    return pl.pallas_call(
        join_kernel,
        out_shape=jax.ShapeDtypeStruct(shape, jnp.bfloat16),
        in_specs=[ANY] * len(pieces),
        out_specs=ANY,
        scratch_shapes=[pltpu.SemaphoreType.DMA((len(pieces),))],
        compiler_params=PARAMS,
        name="join",
    )(*pieces)


def mask_kernel(owners, offsets, pattern, factor, masked):
    start = own_start(owners, offsets)
    position = lax.axis_index("row")
    owned = jnp.int32(SN)
    for node in range(SN):
        owned = jnp.where(owners[node] == position, node, owned)
    for top in range(0, factor.shape[0], BLK):
        rank = jnp.where((top >= start) & (top < start + SNR), owned, SN)
        for col in range(0, factor.shape[1], BLK):
            keep = (pattern[top // BLK, col // BLK] > 0) & (rank > col // SNR)
            tile = factor[top : top + BLK, col : col + BLK]
            masked[top : top + BLK, col : col + BLK] = jnp.where(keep, tile, jnp.zeros_like(tile))


def mask(owners, offsets, pattern, factor):
    return pl.pallas_call(
        mask_kernel,
        out_shape=jax.ShapeDtypeStruct(factor.shape, factor.dtype),
        in_specs=[SMEM] * 3 + [pl.BlockSpec(memory_space=pltpu.VMEM)],
        out_specs=pl.BlockSpec(memory_space=pltpu.VMEM),
        compiler_params=PARAMS,
        name="mask",
    )(owners, offsets, pattern, factor)


def first_kernel(n_row, held, owners, inverse, masked, right, *refs):
    slots = fill(held, refs[: sum(held)])
    segments, solution, total, segment, sems = refs[sum(held) :]

    def place(node, slot):
        target = segments.at[node - 1] if node else segment
        return pltpu.make_async_copy(slot, target, sems.at[node])

    for node in range(SN):
        start_matching(slots, slot_of(owners[node], n_row), functools.partial(place, node))
    place(0, slots[0]).wait()
    x = jnp.dot(inverse[0], segment[...], preferred_element_type=jnp.float32).astype(jnp.bfloat16)
    solution[...] = x
    update = jnp.dot(masked[:, :SNR], x, preferred_element_type=jnp.float32)
    total[...] = right[...].astype(jnp.float32) - update
    for node in range(1, SN):
        place(node, slots[0]).wait()


def first(owners, inverse, masked, right, slots, n_row):
    held = [slot is not None for slot in slots]
    rows, columns = right.shape
    return pl.pallas_call(
        functools.partial(first_kernel, n_row, held),
        out_shape=(
            jax.ShapeDtypeStruct((SN - 1, SNR, columns), jnp.bfloat16),
            jax.ShapeDtypeStruct((SNR, columns), jnp.bfloat16),
            jax.ShapeDtypeStruct((rows, columns), jnp.float32),
        ),
        in_specs=[SMEM] + [VMEM] * 3 + [ANY] * sum(held),
        out_specs=(ANY, VMEM, VMEM),
        scratch_shapes=[
            pltpu.VMEM((SNR, columns), jnp.bfloat16),
            pltpu.SemaphoreType.DMA((SN,)),
        ],
        compiler_params=PARAMS,
        cost_estimate=pl.CostEstimate(flops=60 * 10**9, bytes_accessed=0, transcendentals=0),
        name="first",
    )(owners, inverse, masked, right, *(slot for slot in slots if slot is not None))


def middle_kernel(inverse, masked, segments, start, before, *refs):
    *pieces, solutions, total, near, sems = refs
    copies = {
        node: join_copies(
            pieces, near, sems.at[node - 1], pl.ds(node * (node - 1) // 2 * SNR, node * SNR)
        )
        for node in range(1, SN - 1)
    }
    for node in copies:
        for copy in copies[node]:
            copy.start()
    left = before[...]
    for node in range(1, SN - 1):
        for copy in copies[node]:
            copy.wait()
        at = node * (node - 1) // 2 * SNR
        update = jnp.dot(near[:, at : at + SNR], start[...], preferred_element_type=jnp.float32)
        if node > 1:
            update += jnp.dot(
                near[:, at + SNR : at + node * SNR],
                solutions[: (node - 1) * SNR],
                preferred_element_type=jnp.float32,
            )
        segment = (segments[node - 1].astype(jnp.float32) - update).astype(jnp.bfloat16)
        x = jnp.dot(inverse[node], segment, preferred_element_type=jnp.float32).astype(jnp.bfloat16)
        solutions[(node - 1) * SNR : node * SNR] = x
    cols = masked[:, SNR : (SN - 1) * SNR]
    total[...] = left - jnp.dot(cols, solutions[...], preferred_element_type=jnp.float32)


def middle(inverse, near, masked, segments, start, total):
    columns = start.shape[1]
    return pl.pallas_call(
        middle_kernel,
        out_shape=(
            jax.ShapeDtypeStruct(((SN - 2) * SNR, columns), jnp.bfloat16),
            jax.ShapeDtypeStruct(total.shape, jnp.float32),
        ),
        in_specs=[VMEM] * 5 + [ANY] * len(near),
        out_specs=(VMEM, VMEM),
        scratch_shapes=[pltpu.VMEM((SNR, near[0].shape[1]), jnp.bfloat16), pltpu.SemaphoreType.DMA((SN - 2, len(near)))],
        compiler_params=PARAMS,
        cost_estimate=pl.CostEstimate(flops=24 * 10**9, bytes_accessed=0, transcendentals=0),
        name="middle",
    )(inverse, masked, segments, start, total, *near)


def last_kernel(inverse, masked, segments, start, solutions, total, *refs):
    *pieces, solved, updated, far, xs, out, sems, far_sems = refs
    copies = [
        join_copies(pieces, far, far_sems.at[i], cols)
        for i, cols in enumerate((pl.ds(0, SNR), pl.ds(SNR, LEFT - SNR)))
    ]
    for copy in copies[0] + copies[1]:
        copy.start()
    position = lax.axis_index("row")
    last = (SN - 1) * SNR
    moves = [
        pltpu.make_async_copy(start, xs.at[pl.ds(0, SNR)], sems.at[0]),
        pltpu.make_async_copy(solutions, xs.at[pl.ds(SNR, last - SNR)], sems.at[1]),
    ]
    for move in moves:
        move.start()
    for copy in copies[0]:
        copy.wait()
    update = jnp.dot(far[:, :SNR], start[...], preferred_element_type=jnp.float32)
    for copy in copies[1]:
        copy.wait()
    update += jnp.dot(far[:, SNR:], solutions[...], preferred_element_type=jnp.float32)
    segment = (segments[SN - 2].astype(jnp.float32) - update).astype(jnp.bfloat16)
    x = jnp.dot(inverse[SN - 1], segment, preferred_element_type=jnp.float32).astype(jnp.bfloat16)
    xs[last:] = x
    for move in moves:
        move.wait()
    out_rows = solved.shape[0]
    solved_copy = pltpu.make_async_copy(
        xs.at[pl.ds(pl.multiple_of(position * out_rows, out_rows), out_rows)], solved, sems.at[0]
    )
    solved_copy.start()
    half = pl.cdiv(total.shape[0] // 2, BLK) * BLK
    copies = [solved_copy]
    for part, rows in enumerate((pl.ds(0, half), pl.ds(half, total.shape[0] - half))):
        update = jnp.dot(masked[rows, last:], x, preferred_element_type=jnp.float32)
        out[rows] = (total[rows] - update).astype(jnp.bfloat16)
        copies.append(pltpu.make_async_copy(out.at[rows], updated.at[rows], sems.at[1 + part]))
        copies[-1].start()
    for copy in copies:
        copy.wait()


def last(inverse, far, masked, segments, start, solutions, total, n_row):
    rows, columns = total.shape
    return pl.pallas_call(
        last_kernel,
        out_shape=(
            jax.ShapeDtypeStruct((SN * SNR // n_row, columns), jnp.bfloat16),
            jax.ShapeDtypeStruct((rows, columns), jnp.bfloat16),
        ),
        in_specs=[VMEM] * 6 + [ANY] * len(far),
        out_specs=(ANY, ANY),
        scratch_shapes=[
            pltpu.VMEM((SNR, LEFT), jnp.bfloat16),
            pltpu.VMEM((SN * SNR, columns), jnp.bfloat16),
            pltpu.VMEM((rows, columns), jnp.bfloat16),
            pltpu.SemaphoreType.DMA((3,)),
            pltpu.SemaphoreType.DMA((2, len(far))),
        ],
        compiler_params=PARAMS,
        name="last",
    )(inverse, masked, segments, start, solutions, total, *far)


def on_device(right_side, factor, pattern, inverses, owners, offsets):
    n_row, n_src = lax.axis_size("row"), lax.axis_size("src")
    piece, segment = stage(owners, offsets, pattern, factor, right_side, n_src)
    pieces = line_gather(piece, n_row)
    inverse = join(src_gather(inverses, n_src))
    near, far = pick(owners, pieces, n_row)
    near, far, inverse = lax.optimization_barrier((near, far, inverse))
    near, far = src_gather(near, n_src), src_gather(far, n_src)
    masked = mask(owners, offsets, pattern, factor)
    slots = line_gather(segment, n_row)
    segments, start, total = first(owners, inverse, masked, right_side, slots, n_row)
    solutions, total = middle(inverse, near, masked, segments, start, total)
    return last(inverse, far, masked, segments, start, solutions, total, n_row)


def solution(mesh):
    placed = (
        P(("group", "row"), "src"),
        P(("group", "row"), None),
        P(("group", "row"), None),
        P("group", "src", None),
        P("group"),
        P("group"),
    )
    return jax.shard_map(
        on_device,
        mesh=mesh,
        in_specs=placed,
        out_specs=(P(("group", "row"), "src"), P(("group", "row"), "src")),
        check_vma=False,
    )
```
